32 devices in a mesh: groups: 2 (over y), wt: 4 (over z), dp: 2 (over x), lin: 2 (over core).
Axes of the slice: x: 2, y: 2, z: 4, core: 2. Of those that a mesh axis runs over, the one named last changes fastest.
Arguments:
- weights: bfloat16 [4, 8192, 8192], P(('groups', 'lin'), 'dp', 'wt'), parts along dimension 0
- codes: int32 [4, 8192, 8192], P(('groups', 'lin'), 'dp', 'wt'), parts along dimension 0, may hold values from 0 to 15, as said below
- scales: float32 [4, 64, 8192], P(('groups', 'lin'), 'wt', 'dp'), parts along dimension 0, may hold values from 0.5 to 5
- tokens: bfloat16 [4096, 8192], P(('groups', 'dp'), 'wt'), parts along dimension 0, may hold values from -6 to 6
- sketch: bfloat16 [4096, 256], P(('groups', 'dp')), parts along dimension 0, may hold values from -6 to 6
Outputs:
- basis: float32 [4, 8192, 256], P(('groups', 'lin'), ('dp', 'wt')), parts along dimension 0
- factor: float32 [4, 8192, 256], P(('groups', 'lin'), 'wt'), parts along dimension 0
The draws below stay inside these ranges and needn't reach their ends.
There are 2 independent parts, one for each index of `groups`. The reference program is written for one: setup_inputs(seed, part) draws one part's arguments, and reference() takes and returns one part's arrays. A program takes and returns all parts, laid end to end along the dimension named above; each array names one. Nothing has to cross between parts.
Inputs may be any that keep to these rules, and one draw needn't show every extreme that they name: codes holds the int4 codes of weights under scales: weights lies within about half a scale of s (codes - 8).
All inputs are finite; a program needn't handle non-finite values.
Results may differ from the reference program's by a relative error of at most 0.03.
Values may be sent and summed in bfloat16 or wider, within the bound.
A program may use at most 192 MiB of HBM per device.

```python
import math
import jax
import jax.numpy as jnp

D = 8192
OUT = 8192
R = 256
G = 128
ITERS = 1
TOK = 2048


def shared_quant(key):
    code_key = jax.random.fold_in(key, 11)
    scale_key = jax.random.fold_in(key, 12)
    codes = jax.random.randint(code_key, (2, OUT, D), 0, 16).astype(jnp.int32)
    spread = jax.random.uniform(scale_key, (2, D // G, OUT), jnp.float32, math.log(0.5), math.log(5.0))
    return (codes, jnp.exp(spread))


def draw_codes(key, part):
    codes, scales = shared_quant(key)
    return codes


def draw_scales(key, part):
    codes, scales = shared_quant(key)
    return scales.astype(jnp.float32)


def draw_weights(key, part):
    codes, scales = shared_quant(key)
    key = jax.random.fold_in(key, 3)
    first = jax.random.uniform(jax.random.fold_in(key, 1), (2, OUT, D), jnp.float32, -0.5, 0.5)
    residual = first
    expanded = jnp.transpose(jnp.repeat(scales, G, axis=1), (0, 2, 1))
    weights = expanded * (codes.astype(jnp.float32) - 8.0 + residual)
    return weights.astype(jnp.bfloat16)


def block_levels(rng, shape, cuts, smallest, largest):
    def one(dim, shards_of):
        steps = jax.random.uniform(jax.random.fold_in(jax.random.fold_in(rng, 6), dim), (shards_of,), jnp.float32, smallest / len(cuts), largest / len(cuts))
        return jnp.repeat(jnp.exp(steps), shape[dim] // shards_of).reshape((-1,) + (1,) * (len(shape) - dim - 1))

    level = one(*cuts[0])
    for cut in cuts[1:]:
        level = level * one(*cut)
    return level


def centred(rng, shape, width, limit, shards=(), held_as=jnp.bfloat16):
    array = jax.random.normal(rng, shape, jnp.float32) * width
    if len(shards) > 0:
        array = block_levels(rng, shape, shards, -0.22, 0.18) * array
    return jnp.clip(array, min=-limit, max=limit).astype(held_as)


def setup_inputs(seed: int = 0, part: int = 0) -> dict:
    arg_keys = jax.random.split(jax.random.key(seed), 6)
    own_keys = jax.random.split(jax.random.fold_in(arg_keys[5], part), 6)
    return {
        "weights": draw_weights(jax.random.fold_in(jax.random.fold_in(arg_keys[5], part), 71), part),
        "codes": draw_codes(jax.random.fold_in(jax.random.fold_in(arg_keys[5], part), 71), part),
        "scales": draw_scales(jax.random.fold_in(jax.random.fold_in(arg_keys[5], part), 71), part),
        "tokens": centred(own_keys[3], (TOK, D), 1.0, 6.0, ((0, 2), (1, 4))),
        "sketch": centred(own_keys[4], (TOK, R), 1.0, 6.0, ((0, 2),)),
    }


def one_linear(weight, code, scale, tokens, sketch):
    expanded = jnp.repeat(scale, G, axis=0).T
    error = (weight.astype(jnp.float32) - expanded * (code.astype(jnp.float32) - 8.0)).astype(jnp.bfloat16)
    moment = jnp.dot(tokens.T.astype(jnp.float32), sketch.astype(jnp.float32), preferred_element_type=jnp.float32).astype(jnp.bfloat16)
    projected = None
    lower = None
    image = None
    for step in range(ITERS + 1):
        image = jnp.dot(error.astype(jnp.float32), moment.astype(jnp.float32), preferred_element_type=jnp.float32).astype(jnp.bfloat16)
        gram = jnp.dot(image.T.astype(jnp.float32), image.astype(jnp.float32), preferred_element_type=jnp.float32)
        lower = jnp.linalg.cholesky(gram)
        panel = jnp.dot(error.T.astype(jnp.float32), image.astype(jnp.float32), preferred_element_type=jnp.float32)
        projected = jax.scipy.linalg.solve_triangular(lower, panel.T, lower=True).T
        if step < ITERS:
            rounded = projected.astype(jnp.bfloat16)
            scores = jnp.dot(tokens.astype(jnp.float32), rounded.astype(jnp.float32), preferred_element_type=jnp.float32).astype(jnp.bfloat16)
            moment = jnp.dot(tokens.T.astype(jnp.float32), scores.astype(jnp.float32), preferred_element_type=jnp.float32).astype(jnp.bfloat16)
    basis = jax.scipy.linalg.solve_triangular(lower, image.astype(jnp.float32).T, lower=True).T * math.sqrt(OUT)
    return (basis, projected)

def reference(weights, codes, scales, tokens, sketch):
    first = one_linear(weights[0], codes[0], scales[0], tokens, sketch)
    second = one_linear(weights[1], codes[1], scales[1], tokens, sketch)
    return (jnp.stack([first[0], second[0]]), jnp.stack([first[1], second[1]]))
```

```python
import functools
import math

import jax
import jax.numpy as jnp
from jax import lax
from jax.experimental import pallas as pl
from jax.experimental.pallas import tpu as pltpu
from jax.sharding import PartitionSpec as P

OUT = 8192
G = 128
ITERS = 1
HIGHEST = lax.Precision.HIGHEST


def cross(left, right):
    return lax.dot_general(
        left, right, (((0,), (0,)), ((), ())), preferred_element_type=jnp.float32
    )


def error_kernel(w_ref, c_ref, s_ref, e_ref):
    scale = s_ref[...]
    for g in range(w_ref.shape[1] // G):
        cols = slice(g * G, (g + 1) * G)
        step = scale[:, g : g + 1] * (c_ref[:, cols].astype(jnp.float32) - 8.0)
        e_ref[:, cols] = (w_ref[:, cols].astype(jnp.float32) - step).astype(jnp.bfloat16)


def quant_error(weights, codes, scales):
    rows, cols = weights.shape
    tile = 256
    return pl.pallas_call(
        error_kernel,
        grid=(rows // tile,),
        in_specs=[
            pl.BlockSpec((tile, cols), lambda i: (i, 0)),
            pl.BlockSpec((tile, cols), lambda i: (i, 0)),
            pl.BlockSpec((tile, cols // G), lambda i: (i, 0)),
        ],
        out_specs=pl.BlockSpec((tile, cols), lambda i: (i, 0)),
        out_shape=jax.ShapeDtypeStruct((rows, cols), jnp.bfloat16),
        compiler_params=pltpu.CompilerParams(vmem_limit_bytes=32 * 2**20),
        cost_estimate=pl.CostEstimate(
            flops=4 * rows * cols, bytes_accessed=8 * rows * cols, transcendentals=0
        ),
        name="quant_error",
    )(weights, codes, scales.T)


def invert_block(a):
    n = a.shape[0]
    lane = lax.broadcasted_iota(jnp.int32, (8, n), 1)
    sub = lax.broadcasted_iota(jnp.int32, (8, n), 0)
    blocks = [a[8 * b : 8 * b + 8, :] for b in range(n // 8)]
    for j in range(n):
        home, r = divmod(j, 8)
        row = blocks[home][r : r + 1, :]
        pivot = jnp.broadcast_to(row[:, j : j + 1], (8, n))
        line = jnp.broadcast_to(row, (8, n))
        line = jnp.where(lane == j, 1.0, line) / pivot
        for b in range(home, n // 8):
            if b == home and r == 7:
                continue
            col = jnp.broadcast_to(blocks[b][:, j : j + 1], (8, n))
            new = jnp.where(lane == j, 0.0, blocks[b]) - col * line
            blocks[b] = jnp.where(sub > r, new, blocks[b]) if b == home else new
    out = []
    for b in range(n // 8):
        index = sub + 8 * b
        diag = jnp.sum(jnp.where(lane == index, blocks[b], 0.0), axis=1, keepdims=True)
        unit = jnp.where(lane < index, blocks[b], jnp.where(lane == index, 1.0, 0.0))
        out.append(unit * lax.rsqrt(diag))
    return jnp.concatenate(out, axis=0)


def dot_hi(left, right, dims):
    return lax.dot_general(
        left, right, (dims, ((), ())), precision=HIGHEST, preferred_element_type=jnp.float32
    )


def invert_kernel(a_ref, o_ref):
    n = a_ref.shape[0]
    h = n // 2
    top = invert_block(a_ref[:h, :h])
    low = dot_hi(a_ref[h:, :h], top, ((1,), (1,)))
    rest = a_ref[h:, h:] - dot_hi(low, low, ((1,), (1,)))
    bottom = invert_block(rest)
    o_ref[:h, :h] = top
    o_ref[:h, h:] = jnp.zeros((h, h), jnp.float32)
    o_ref[h:, h:] = bottom
    o_ref[h:, :h] = -dot_hi(bottom, dot_hi(low, top, ((1,), (0,))), ((1,), (0,)))


def inverse_factor(gram):
    n = gram.shape[0]
    return pl.pallas_call(
        invert_kernel,
        out_shape=jax.ShapeDtypeStruct((n, n), jnp.float32),
        compiler_params=pltpu.CompilerParams(vmem_limit_bytes=16 * 2**20),
        cost_estimate=pl.CostEstimate(
            flops=40 * 10**9, bytes_accessed=2 * 4 * n * n, transcendentals=0
        ),
        name="inverse_factor",
    )(gram)


def local(dp, weights, codes, scales, tokens, sketch):
    pairs = [(i, (i + s) % dp) for s in range(1, dp) for i in range(dp)]

    def dp_sum(part):
        if dp == 2:
            other = lax.ppermute(part, "dp", pairs)
            return part.astype(jnp.float32) + other.astype(jnp.float32)
        return lax.psum(part.astype(jnp.float32), "dp")

    def token_moment(vectors):
        part = cross(tokens, vectors).astype(jnp.bfloat16)
        return dp_sum(part).astype(jnp.bfloat16)

    moment = token_moment(sketch)
    error = quant_error(weights[0], codes[0], scales[0])
    rounded = None
    projected = None
    for step in range(ITERS + 1):
        part = jnp.dot(error, moment, preferred_element_type=jnp.float32).astype(jnp.bfloat16)
        share = lax.psum_scatter(part, "wt", scatter_dimension=0, tiled=True)
        image = lax.all_gather(share, "wt", axis=0, tiled=True)
        gram = dp_sum(cross(image, image))
        panel = dp_sum(cross(error, image).astype(jnp.bfloat16))
        inverse = inverse_factor(gram)
        projected = dot_hi(panel, inverse, ((1,), (1,)))
        if step < ITERS:
            rounded = projected.astype(jnp.bfloat16)
            scores = jnp.dot(tokens, rounded, preferred_element_type=jnp.float32)
            scores = lax.psum(scores.astype(jnp.bfloat16), "wt")
            moment = token_moment(scores)
    basis = dot_hi(share.astype(jnp.float32), inverse * math.sqrt(OUT), ((1,), (1,)))
    return (basis[None], projected[None])


def solution(mesh):
    placed = (
        P(("groups", "lin"), "dp", "wt"),
        P(("groups", "lin"), "dp", "wt"),
        P(("groups", "lin"), "wt", "dp"),
        P(("groups", "dp"), "wt"),
        P(("groups", "dp"), None),
    )
    return jax.shard_map(
        functools.partial(local, mesh.shape["dp"]),
        mesh=mesh,
        in_specs=placed,
        out_specs=(P(("groups", "lin"), ("dp", "wt"), None), P(("groups", "lin"), "wt", None)),
        check_vma=False,
    )
```

```python
import functools
import math

import jax
import jax.numpy as jnp
from jax import lax
from jax.experimental import pallas as pl
from jax.experimental.pallas import tpu as pltpu
from jax.sharding import PartitionSpec as P

OUT = 8192
G = 128
ITERS = 1
HIGHEST = lax.Precision.HIGHEST


def cross(left, right):
    return lax.dot_general(
        left, right, (((0,), (0,)), ((), ())), preferred_element_type=jnp.float32
    )


def error_kernel(w_ref, c_ref, s_ref, e_ref):
    scale = s_ref[...]
    for g in range(w_ref.shape[1] // G):
        cols = slice(g * G, (g + 1) * G)
        step = scale[:, g : g + 1] * (c_ref[:, cols].astype(jnp.float32) - 8.0)
        e_ref[:, cols] = (w_ref[:, cols].astype(jnp.float32) - step).astype(jnp.bfloat16)


def quant_error(weights, codes, scales):
    rows, cols = weights.shape
    tile = 256
    return pl.pallas_call(
        error_kernel,
        grid=(rows // tile,),
        in_specs=[
            pl.BlockSpec((tile, cols), lambda i: (i, 0)),
            pl.BlockSpec((tile, cols), lambda i: (i, 0)),
            pl.BlockSpec((tile, cols // G), lambda i: (i, 0)),
        ],
        out_specs=pl.BlockSpec((tile, cols), lambda i: (i, 0)),
        out_shape=jax.ShapeDtypeStruct((rows, cols), jnp.bfloat16),
        compiler_params=pltpu.CompilerParams(vmem_limit_bytes=32 * 2**20),
        cost_estimate=pl.CostEstimate(
            flops=4 * rows * cols, bytes_accessed=8 * rows * cols, transcendentals=0
        ),
        name="quant_error",
    )(weights, codes, scales.T)


def invert_block(a):
    n = a.shape[0]
    lane = lax.broadcasted_iota(jnp.int32, (8, n), 1)
    sub = lax.broadcasted_iota(jnp.int32, (8, n), 0)
    blocks = [a[8 * b : 8 * b + 8, :] for b in range(n // 8)]
    for j in range(n):
        home, r = divmod(j, 8)
        row = blocks[home][r : r + 1, :]
        pivot = jnp.broadcast_to(row[:, j : j + 1], (8, n))
        line = jnp.broadcast_to(row, (8, n))
        line = jnp.where(lane == j, 1.0, line) / pivot
        for b in range(home, n // 8):
            if b == home and r == 7:
                continue
            col = jnp.broadcast_to(blocks[b][:, j : j + 1], (8, n))
            new = jnp.where(lane == j, 0.0, blocks[b]) - col * line
            blocks[b] = jnp.where(sub > r, new, blocks[b]) if b == home else new
    out = []
    for b in range(n // 8):
        index = sub + 8 * b
        diag = jnp.sum(jnp.where(lane == index, blocks[b], 0.0), axis=1, keepdims=True)
        unit = jnp.where(lane < index, blocks[b], jnp.where(lane == index, 1.0, 0.0))
        out.append(unit * lax.rsqrt(diag))
    return jnp.concatenate(out, axis=0)


def dot_hi(left, right, dims):
    return lax.dot_general(
        left, right, (dims, ((), ())), precision=HIGHEST, preferred_element_type=jnp.float32
    )


def invert_kernel(a_ref, o_ref):
    n = a_ref.shape[0]
    h = n // 2
    top = invert_block(a_ref[:h, :h])
    low = dot_hi(a_ref[h:, :h], top, ((1,), (1,)))
    rest = a_ref[h:, h:] - dot_hi(low, low, ((1,), (1,)))
    bottom = invert_block(rest)
    o_ref[:h, :h] = top
    o_ref[:h, h:] = jnp.zeros((h, h), jnp.float32)
    o_ref[h:, h:] = bottom
    o_ref[h:, :h] = -dot_hi(bottom, dot_hi(low, top, ((1,), (0,))), ((1,), (0,)))


def inverse_factor(gram):
    n = gram.shape[0]
    return pl.pallas_call(
        invert_kernel,
        out_shape=jax.ShapeDtypeStruct((n, n), jnp.float32),
        compiler_params=pltpu.CompilerParams(vmem_limit_bytes=16 * 2**20),
        cost_estimate=pl.CostEstimate(
            flops=40 * 10**9, bytes_accessed=2 * 4 * n * n, transcendentals=0
        ),
        name="inverse_factor",
    )(gram)


PIECES = 16


def image_kernel(
    e_ref, m_ref, image_ref, panel_ref, gram_ref,
    stage, outer_in, inner_in, final, total,
    s_part, r_outer, s_in, r_in, s_fin_in, s_fin_out, r_fin,
):
    me = lax.axis_index("wt")
    half = PIECES // 2
    size = e_ref.shape[0] // PIECES
    low = me < 2
    is_end = (me == 0) | (me == 3)
    middle = jnp.where(low, 1, 2)
    outer = jnp.where(low, 0, 3)
    inner = jnp.where(low, 2, 1)
    mine = jnp.where(low, 0, half)
    other = half - mine
    barrier = pltpu.get_barrier_semaphore()

    def rows(p):
        return pl.ds(pl.multiple_of(p * size, size), size)

    def copy(src, dst, send, recv, target):
        return pltpu.make_async_remote_copy(
            src_ref=src, dst_ref=dst, send_sem=send, recv_sem=recv,
            device_id={"wt": target}, device_id_type=pl.DeviceIdType.MESH,
        )

    def part_copy(p):
        return copy(stage.at[p], outer_in.at[p], s_part.at[p], r_outer.at[p], middle)

    def in_copy(p, k):
        return copy(stage.at[p], inner_in.at[k], s_in.at[k], r_in.at[k], inner)

    def fin_in_copy(p, k):
        return copy(final.at[p], final.at[p], s_fin_in.at[k], r_fin.at[p], inner)

    def fin_out_copy(p, target):
        return copy(final.at[p], final.at[p], s_fin_out.at[p], r_fin.at[p], target)

    def own(p):
        return jnp.dot(e_ref[rows(p), :], m_ref[...], preferred_element_type=jnp.float32)

    def consume(p):
        piece = final[p]
        image_ref[rows(p), :] = piece
        total[...] += cross(piece, e_ref[rows(p), :])
        gram_ref[...] += cross(piece, piece)

    def greet(target):
        pl.semaphore_signal(
            barrier, inc=1, device_id={"wt": target}, device_id_type=pl.DeviceIdType.MESH
        )

    total[...] = jnp.zeros_like(total)
    gram_ref[...] = jnp.zeros_like(gram_ref)

    @pl.when(is_end)
    def _():
        greet(middle)
        pl.semaphore_wait(barrier, 1)

        @pl.loop(0, PIECES)
        def _(t):
            p = jnp.where(lax.rem(t, 2) == 0, other, mine) + lax.div(t, 2)
            stage[p] = own(p).astype(jnp.bfloat16)
            part_copy(p).start()

        @pl.loop(0, PIECES)
        def _(t):
            p = jnp.where(lax.rem(t, 2) == 0, mine, other) + lax.div(t, 2)
            fin_out_copy(p, middle).wait_recv()
            consume(p)

        @pl.loop(0, PIECES)
        def _(p):
            part_copy(p).wait_send()

    @pl.when(jnp.logical_not(is_end))
    def _():
        greet(outer)
        greet(inner)
        pl.semaphore_wait(barrier, 2)

        def forward(k):
            o = other + k
            fin_in_copy(o, k).wait_recv()
            fin_out_copy(o, outer).start()
            consume(o)

        @pl.loop(0, half)
        def _(k):
            o, m = other + k, mine + k
            left = own(o)
            part_copy(o).wait_recv()
            stage[o] = (left + outer_in[o].astype(jnp.float32)).astype(jnp.bfloat16)
            in_copy(o, k).start()
            left = own(m)
            part_copy(m).wait_recv()
            left = left + outer_in[m].astype(jnp.float32)
            in_copy(m, k).wait_recv()
            final[m] = (left + inner_in[k].astype(jnp.float32)).astype(jnp.bfloat16)
            fin_in_copy(m, k).start()
            fin_out_copy(m, outer).start()
            consume(m)

            @pl.when(k > 0)
            def _():
                forward(k - 1)

        forward(half - 1)

        @pl.loop(0, half)
        def _(k):
            in_copy(other + k, k).wait_send()
            fin_in_copy(mine + k, k).wait_send()

        @pl.loop(0, PIECES)
        def _(p):
            fin_out_copy(p, outer).wait_send()

    panel_ref[...] = total[...].astype(jnp.bfloat16)


def image_step(error, moment, step):
    rows, cols = error.shape
    rank = moment.shape[1]
    size, half = rows // PIECES, PIECES // 2
    dma = pltpu.SemaphoreType.DMA
    vmem = pl.BlockSpec(memory_space=pltpu.VMEM)
    return pl.pallas_call(
        image_kernel,
        in_specs=[vmem, vmem],
        out_specs=[vmem, vmem, vmem],
        out_shape=[
            jax.ShapeDtypeStruct((rows, rank), jnp.bfloat16),
            jax.ShapeDtypeStruct((rank, cols), jnp.bfloat16),
            jax.ShapeDtypeStruct((rank, rank), jnp.float32),
        ],
        scratch_shapes=[
            pltpu.VMEM((PIECES, size, rank), jnp.bfloat16),
            pltpu.VMEM((PIECES, size, rank), jnp.bfloat16),
            pltpu.VMEM((half, size, rank), jnp.bfloat16),
            pltpu.VMEM((PIECES, size, rank), jnp.bfloat16),
            pltpu.VMEM((rank, cols), jnp.float32),
            dma((PIECES,)), dma((PIECES,)), dma((half,)), dma((half,)),
            dma((half,)), dma((PIECES,)), dma((PIECES,)),
        ],
        compiler_params=pltpu.CompilerParams(
            collective_id=step, has_side_effects=True, vmem_limit_bytes=48 * 2**20
        ),
        cost_estimate=pl.CostEstimate(
            flops=60 * 10**9, bytes_accessed=2 * rows * cols, transcendentals=0
        ),
        name="image_step",
    )(error, moment)


def local(dp, wt, weights, codes, scales, tokens, sketch):
    pairs = [(i, (i + s) % dp) for s in range(1, dp) for i in range(dp)]

    def dp_sum(part):
        if dp == 2:
            other = lax.ppermute(part, "dp", pairs)
            return part.astype(jnp.float32) + other.astype(jnp.float32)
        return lax.psum(part.astype(jnp.float32), "dp")

    def token_moment(vectors):
        part = cross(tokens, vectors).astype(jnp.bfloat16)
        return dp_sum(part).astype(jnp.bfloat16)

    moment = token_moment(sketch)
    error = quant_error(weights[0], codes[0], scales[0])
    rounded = None
    projected = None
    for step in range(ITERS + 1):
        if wt == 4:
            image, panel, gram = image_step(error, moment, step)
            start = lax.axis_index("wt") * (image.shape[0] // wt)
            share = lax.dynamic_slice_in_dim(image, start, image.shape[0] // wt)
        else:
            part = jnp.dot(error, moment, preferred_element_type=jnp.float32)
            share = lax.psum_scatter(
                part.astype(jnp.bfloat16), "wt", scatter_dimension=0, tiled=True
            )
            image = lax.all_gather(share, "wt", axis=0, tiled=True)
            gram = cross(image, image)
            panel = cross(image, error).astype(jnp.bfloat16)
        gram = dp_sum(gram)
        panel = dp_sum(panel)
        inverse = inverse_factor(gram)
        projected = dot_hi(panel, inverse, ((0,), (1,)))
        if step < ITERS:
            rounded = projected.astype(jnp.bfloat16)
            scores = jnp.dot(tokens, rounded, preferred_element_type=jnp.float32)
            scores = lax.psum(scores.astype(jnp.bfloat16), "wt")
            moment = token_moment(scores)
    basis = dot_hi(share.astype(jnp.float32), inverse * math.sqrt(OUT), ((1,), (1,)))
    return (basis[None], projected[None])


def solution(mesh):
    placed = (
        P(("groups", "lin"), "dp", "wt"),
        P(("groups", "lin"), "dp", "wt"),
        P(("groups", "lin"), "wt", "dp"),
        P(("groups", "dp"), "wt"),
        P(("groups", "dp"), None),
    )
    return jax.shard_map(
        functools.partial(local, mesh.shape["dp"], mesh.shape["wt"]),
        mesh=mesh,
        in_specs=placed,
        out_specs=(P(("groups", "lin"), ("dp", "wt"), None), P(("groups", "lin"), "wt", None)),
        check_vma=False,
    )
```

```python
import functools
import math

import jax
import jax.numpy as jnp
from jax import lax
from jax.experimental import pallas as pl
from jax.experimental.pallas import tpu as pltpu
from jax.sharding import PartitionSpec as P

OUT = 8192
G = 128
ITERS = 1
HIGHEST = lax.Precision.HIGHEST


def cross(left, right):
    return lax.dot_general(
        left, right, (((0,), (0,)), ((), ())), preferred_element_type=jnp.float32
    )


def error_kernel(w_ref, c_ref, s_ref, e_ref):
    scale = s_ref[...]
    for g in range(w_ref.shape[1] // G):
        cols = slice(g * G, (g + 1) * G)
        step = scale[:, g : g + 1] * (c_ref[:, cols].astype(jnp.float32) - 8.0)
        e_ref[:, cols] = (w_ref[:, cols].astype(jnp.float32) - step).astype(jnp.bfloat16)


def quant_error(weights, codes, scales):
    rows, cols = weights.shape
    tile = 256
    return pl.pallas_call(
        error_kernel,
        grid=(rows // tile,),
        in_specs=[
            pl.BlockSpec((tile, cols), lambda i: (i, 0)),
            pl.BlockSpec((tile, cols), lambda i: (i, 0)),
            pl.BlockSpec((tile, cols // G), lambda i: (i, 0)),
        ],
        out_specs=pl.BlockSpec((tile, cols), lambda i: (i, 0)),
        out_shape=jax.ShapeDtypeStruct((rows, cols), jnp.bfloat16),
        compiler_params=pltpu.CompilerParams(vmem_limit_bytes=32 * 2**20),
        cost_estimate=pl.CostEstimate(
            flops=4 * rows * cols, bytes_accessed=8 * rows * cols, transcendentals=0
        ),
        name="quant_error",
    )(weights, codes, scales.T)


def invert_block(a):
    n = a.shape[0]
    lane = lax.broadcasted_iota(jnp.int32, (8, n), 1)
    sub = lax.broadcasted_iota(jnp.int32, (8, n), 0)
    blocks = [a[8 * b : 8 * b + 8, :] for b in range(n // 8)]
    for j in range(n):
        home, r = divmod(j, 8)
        row = blocks[home][r : r + 1, :]
        pivot = jnp.broadcast_to(row[:, j : j + 1], (8, n))
        line = jnp.broadcast_to(row, (8, n))
        line = jnp.where(lane == j, 1.0, line) / pivot
        for b in range(home, n // 8):
            if b == home and r == 7:
                continue
            col = jnp.broadcast_to(blocks[b][:, j : j + 1], (8, n))
            new = jnp.where(lane == j, 0.0, blocks[b]) - col * line
            blocks[b] = jnp.where(sub > r, new, blocks[b]) if b == home else new
    out = []
    for b in range(n // 8):
        index = sub + 8 * b
        diag = jnp.sum(jnp.where(lane == index, blocks[b], 0.0), axis=1, keepdims=True)
        unit = jnp.where(lane < index, blocks[b], jnp.where(lane == index, 1.0, 0.0))
        out.append(unit * lax.rsqrt(diag))
    return jnp.concatenate(out, axis=0)


def dot_hi(left, right, dims):
    return lax.dot_general(
        left, right, (dims, ((), ())), precision=HIGHEST, preferred_element_type=jnp.float32
    )


def invert_kernel(a_ref, o_ref):
    n = a_ref.shape[0]
    h = n // 2
    top = invert_block(a_ref[:h, :h])
    low = dot_hi(a_ref[h:, :h], top, ((1,), (1,)))
    rest = a_ref[h:, h:] - dot_hi(low, low, ((1,), (1,)))
    bottom = invert_block(rest)
    o_ref[:h, :h] = top
    o_ref[:h, h:] = jnp.zeros((h, h), jnp.float32)
    o_ref[h:, h:] = bottom
    o_ref[h:, :h] = -dot_hi(bottom, dot_hi(low, top, ((1,), (0,))), ((1,), (0,)))


def inverse_factor(gram):
    n = gram.shape[0]
    return pl.pallas_call(
        invert_kernel,
        out_shape=jax.ShapeDtypeStruct((n, n), jnp.float32),
        compiler_params=pltpu.CompilerParams(vmem_limit_bytes=16 * 2**20),
        cost_estimate=pl.CostEstimate(
            flops=40 * 10**9, bytes_accessed=2 * 4 * n * n, transcendentals=0
        ),
        name="inverse_factor",
    )(gram)


PIECES = 16


def image_kernel(
    e_ref, m_ref, image_ref, panel_ref, gram_ref,
    stage, outer_in, inner_in, final, total,
    s_part, r_outer, s_in, r_in, s_fin_in, s_fin_out, r_fin,
):
    me = lax.axis_index("wt")
    pieces = stage.shape[0]
    half = pieces // 2
    size = e_ref.shape[0] // pieces
    low = me < 2
    is_end = (me == 0) | (me == 3)
    middle = jnp.where(low, 1, 2)
    outer = jnp.where(low, 0, 3)
    inner = jnp.where(low, 2, 1)
    mine = jnp.where(low, 0, half)
    other = half - mine
    barrier = pltpu.get_barrier_semaphore()

    def rows(p):
        return pl.ds(pl.multiple_of(p * size, size), size)

    def copy(src, dst, send, recv, target):
        return pltpu.make_async_remote_copy(
            src_ref=src, dst_ref=dst, send_sem=send, recv_sem=recv,
            device_id={"wt": target}, device_id_type=pl.DeviceIdType.MESH,
        )

    def part_copy(p):
        return copy(stage.at[p], outer_in.at[p], s_part.at[p], r_outer.at[p], middle)

    def in_copy(p, k):
        return copy(stage.at[p], inner_in.at[k], s_in.at[k], r_in.at[k], inner)

    def fin_in_copy(p, k):
        return copy(final.at[p], final.at[p], s_fin_in.at[k], r_fin.at[p], inner)

    def fin_out_copy(p, target):
        return copy(final.at[p], final.at[p], s_fin_out.at[p], r_fin.at[p], target)

    def own(p):
        return jnp.dot(e_ref[rows(p), :], m_ref[...], preferred_element_type=jnp.float32)

    def consume(p):
        piece = final[p]
        image_ref[rows(p), :] = piece
        total[...] += cross(piece, e_ref[rows(p), :])
        gram_ref[...] += cross(piece, piece)

    def greet(target):
        pl.semaphore_signal(
            barrier, inc=1, device_id={"wt": target}, device_id_type=pl.DeviceIdType.MESH
        )

    total[...] = jnp.zeros_like(total)
    gram_ref[...] = jnp.zeros_like(gram_ref)

    @pl.when(is_end)
    def _():
        greet(middle)
        pl.semaphore_wait(barrier, 1)

        @pl.loop(0, pieces)
        def _(t):
            p = jnp.where(lax.rem(t, 2) == 0, other, mine) + lax.div(t, 2)
            stage[p] = own(p).astype(jnp.bfloat16)
            part_copy(p).start()

        @pl.loop(0, pieces)
        def _(t):
            p = jnp.where(lax.rem(t, 2) == 0, mine, other) + lax.div(t, 2)
            fin_out_copy(p, middle).wait_recv()
            consume(p)

        @pl.loop(0, pieces)
        def _(p):
            part_copy(p).wait_send()

    @pl.when(jnp.logical_not(is_end))
    def _():
        greet(outer)
        greet(inner)
        pl.semaphore_wait(barrier, 2)

        def forward(k):
            o = other + k
            fin_in_copy(o, k).wait_recv()
            fin_out_copy(o, outer).start()
            consume(o)

        @pl.loop(0, half)
        def _(k):
            o, m = other + k, mine + k
            left = own(o)
            part_copy(o).wait_recv()
            stage[o] = (left + outer_in[o].astype(jnp.float32)).astype(jnp.bfloat16)
            in_copy(o, k).start()
            left = own(m)
            part_copy(m).wait_recv()
            left = left + outer_in[m].astype(jnp.float32)
            in_copy(m, k).wait_recv()
            final[m] = (left + inner_in[k].astype(jnp.float32)).astype(jnp.bfloat16)
            fin_in_copy(m, k).start()
            fin_out_copy(m, outer).start()
            consume(m)

            @pl.when(k > 0)
            def _():
                forward(k - 1)

        forward(half - 1)

        @pl.loop(0, half)
        def _(k):
            in_copy(other + k, k).wait_send()
            fin_in_copy(mine + k, k).wait_send()

        @pl.loop(0, pieces)
        def _(p):
            fin_out_copy(p, outer).wait_send()

    panel_ref[...] = total[...].astype(jnp.bfloat16)


def image_step(error, moment, step, pieces):
    rows, cols = error.shape
    rank = moment.shape[1]
    size, half = rows // pieces, pieces // 2
    dma = pltpu.SemaphoreType.DMA
    vmem = pl.BlockSpec(memory_space=pltpu.VMEM)
    return pl.pallas_call(
        image_kernel,
        in_specs=[vmem, vmem],
        out_specs=[vmem, vmem, vmem],
        out_shape=[
            jax.ShapeDtypeStruct((rows, rank), jnp.bfloat16),
            jax.ShapeDtypeStruct((rank, cols), jnp.bfloat16),
            jax.ShapeDtypeStruct((rank, rank), jnp.float32),
        ],
        scratch_shapes=[
            pltpu.VMEM((pieces, size, rank), jnp.bfloat16),
            pltpu.VMEM((pieces, size, rank), jnp.bfloat16),
            pltpu.VMEM((half, size, rank), jnp.bfloat16),
            pltpu.VMEM((pieces, size, rank), jnp.bfloat16),
            pltpu.VMEM((rank, cols), jnp.float32),
            dma((pieces,)), dma((pieces,)), dma((half,)), dma((half,)),
            dma((half,)), dma((pieces,)), dma((pieces,)),
        ],
        compiler_params=pltpu.CompilerParams(
            collective_id=step, has_side_effects=True, vmem_limit_bytes=48 * 2**20
        ),
        cost_estimate=pl.CostEstimate(
            flops=60 * 10**9, bytes_accessed=2 * rows * cols, transcendentals=0
        ),
        name="image_step",
    )(error, moment)


def local(dp, wt, weights, codes, scales, tokens, sketch):
    pairs = [(i, (i + s) % dp) for s in range(1, dp) for i in range(dp)]

    def dp_sum(part):
        if dp == 2:
            other = lax.ppermute(part, "dp", pairs)
            return part.astype(jnp.float32) + other.astype(jnp.float32)
        return lax.psum(part.astype(jnp.float32), "dp")

    def token_moment(vectors):
        part = cross(tokens, vectors).astype(jnp.bfloat16)
        return dp_sum(part).astype(jnp.bfloat16)

    moment = token_moment(sketch)
    error = quant_error(weights[0], codes[0], scales[0])
    rounded = None
    projected = None
    for step in range(ITERS + 1):
        if wt == 4:
            image, panel, gram = image_step(error, moment, step, PIECES)
            start = lax.axis_index("wt") * (image.shape[0] // wt)
            share = lax.dynamic_slice_in_dim(image, start, image.shape[0] // wt)
        else:
            part = jnp.dot(error, moment, preferred_element_type=jnp.float32)
            share = lax.psum_scatter(
                part.astype(jnp.bfloat16), "wt", scatter_dimension=0, tiled=True
            )
            image = lax.all_gather(share, "wt", axis=0, tiled=True)
            gram = cross(image, image)
            panel = cross(image, error).astype(jnp.bfloat16)
        gram = dp_sum(gram)
        panel = dp_sum(panel)
        inverse = inverse_factor(gram)
        projected = dot_hi(panel, inverse, ((0,), (1,)))
        if step < ITERS:
            rounded = projected.astype(jnp.bfloat16)
            if wt == 4:
                _, part, _ = image_step(tokens, rounded, ITERS + 1 + step, PIECES // 2)
                moment = dp_sum(part).T.astype(jnp.bfloat16)
            else:
                scores = jnp.dot(tokens, rounded, preferred_element_type=jnp.float32)
                scores = lax.psum(scores.astype(jnp.bfloat16), "wt")
                moment = token_moment(scores)
    basis = dot_hi(share.astype(jnp.float32), inverse * math.sqrt(OUT), ((1,), (1,)))
    return (basis[None], projected[None])


def solution(mesh):
    placed = (
        P(("groups", "lin"), "dp", "wt"),
        P(("groups", "lin"), "dp", "wt"),
        P(("groups", "lin"), "wt", "dp"),
        P(("groups", "dp"), "wt"),
        P(("groups", "dp"), None),
    )
    return jax.shard_map(
        functools.partial(local, mesh.shape["dp"], mesh.shape["wt"]),
        mesh=mesh,
        in_specs=placed,
        out_specs=(P(("groups", "lin"), ("dp", "wt"), None), P(("groups", "lin"), "wt", None)),
        check_vma=False,
    )
```
